32 devices in a mesh: grp: 4 (over x, core), mem: 8 (over z, y).
Axes of the slice: x: 2, y: 2, z: 4, core: 2. Of those that a mesh axis runs over, the one named last changes fastest.
Arguments:
- clips: bfloat16 [8192, 1152], P(('grp', 'mem')), may hold values from -6 to 6
- captions: bfloat16 [2048, 1152], P(('grp', 'mem')), may hold values from -6 to 6
- clip_bucket: int32 [8192], P(('grp', 'mem')), may hold values from 0 to 7, as said below
- clip_positive: int32 [8192], P(('grp', 'mem')), may hold values from 0 to 2047, as said below
- caption_bucket: int32 [2048], P(('grp', 'mem')), may hold values from 0 to 7, as said below
- bucket_owner: int32 [8], replicated, may hold values from 0 to 3, as said below
- scale: float32 [1], replicated, may hold values from 0.02 to 0.06
- bias: float32 [1], replicated, may hold values from -4 to -1
Outputs:
- clip_grad: float32 [8192, 1152], P(('grp', 'mem'))
- caption_grad: float32 [2048, 1152], P(('grp', 'mem'))
The draws below stay inside these ranges and needn't reach their ends.
Inputs may be any that keep to these rules, and one draw needn't show every extreme that they name: `bucket_owner`: each group owns exactly 2 buckets. `caption_bucket`: caption rows g * 512 to (g + 1) * 512 - 1 have buckets owned by group g, and every bucket has a caption. `clip_bucket`: within one device's block of 256 clip rows, among the rows whose offsets in the block are equal modulo the size of axis mem, at most 16 have buckets owned by one group; one group receives exactly 16 such rows from every such set of every device. `clip_positive`: each clip's own caption has the clip's bucket.
All inputs are finite; a program needn't handle non-finite values.
Results may differ from the reference program's by a relative error of at most 0.0027.
Values may be sent and summed in bfloat16 or wider, within the bound.
A program may use at most 128 MiB of HBM per device.

```python
import math
import jax
import jax.numpy as jnp
from jax import lax

D = 1152
CLIP_DEV = 256
BPG = 2
CLIPS = 8192
CAPTIONS = 2048
PANEL = 512
BUCKETS = 8
CAP = 16
SLOTS = 512
N_GRP = 4
N_MEM = 8


def layout(key):
    key_owner = jax.random.fold_in(key, 101)
    key_caption = jax.random.fold_in(key, 202)
    key_favored = jax.random.fold_in(key, 303)
    key_rank = jax.random.fold_in(key, 404)
    key_mix = jax.random.fold_in(key, 505)
    key_positive = jax.random.fold_in(key, 606)
    shuffled = jax.random.permutation(key_owner, BUCKETS).astype(jnp.int32)
    owner = (shuffled // BPG).astype(jnp.int32)
    slot_bucket = jnp.argsort(shuffled).astype(jnp.int32)
    cap_rows = jnp.arange(CAPTIONS, dtype=jnp.int32)
    within = cap_rows % PANEL
    picked = jax.random.randint(key_caption, (CAPTIONS,), 0, BPG, dtype=jnp.int32)
    local_slot = jnp.where(within < BPG, within, picked)
    caption_bucket = slot_bucket[cap_rows // PANEL * BPG + local_slot]
    devices = N_GRP * N_MEM
    per_lane = CLIP_DEV // N_MEM
    slot_count = N_GRP * CAP
    lanes = devices * N_MEM
    favored = jax.random.randint(key_favored, (), 0, N_GRP, dtype=jnp.int32)
    slot_ids = jnp.arange(slot_count, dtype=jnp.int32)
    noise = jax.random.randint(key_rank, (lanes, slot_count), 0, 1 << 20, dtype=jnp.int32)
    score = noise * slot_count + slot_ids[None, :]
    score = jnp.where((slot_ids // CAP == favored)[None, :], slot_ids[None, :] - slot_count, score)
    chosen = jnp.argsort(score, axis=1)[:, :per_lane].astype(jnp.int32)
    mixing = jax.random.randint(key_mix, (lanes, per_lane), 0, 1 << 20, dtype=jnp.int32)
    mixing = mixing * per_lane + jnp.arange(per_lane, dtype=jnp.int32)[None, :]
    chosen = jnp.take_along_axis(chosen, jnp.argsort(mixing, axis=1), axis=1)
    group = (chosen // CAP).astype(jnp.int32)
    group = group.reshape(devices, N_MEM, per_lane).transpose(0, 2, 1).reshape(CLIPS)
    offset = jax.random.randint(key_positive, (CLIPS,), 0, PANEL, dtype=jnp.int32)
    positive = (group * PANEL + offset).astype(jnp.int32)
    clip_bucket = caption_bucket[positive]
    return (owner, caption_bucket, clip_bucket, positive)


def draw_bucket_owner(key, part):
    return layout(key)[0]


def draw_caption_bucket(key, part):
    return layout(key)[1]


def draw_clip_bucket(key, part):
    return layout(key)[2]


def draw_clip_positive(key, part):
    return layout(key)[3]


def shard_levels(stream_key, shape, cuts, smallest, top_value):
    factor_of, own = 1.0, jax.random.fold_in(stream_key, 6)
    for axis_at, shards_of in cuts:
        draws = jnp.exp(jax.random.uniform(jax.random.fold_in(own, axis_at), (shards_of,), jnp.float32, smallest / len(cuts), top_value / len(cuts)))
        factor_of = factor_of * jnp.repeat(draws, shape[axis_at] // shards_of).reshape([-1 if axis == axis_at else 1 for axis in range(len(shape))])
    return factor_of


def normal_values(key, dims, scale, reach, cuts=(), held_as=jnp.bfloat16):
    level = shard_levels(key, dims, cuts, -0.22, 0.18) if cuts else 1.0
    drawn = jax.random.normal(key, dims, jnp.float32) * scale * level
    return jnp.minimum(jnp.maximum(drawn, -reach), reach).astype(held_as)


def setup_inputs(seed: int = 0) -> dict:
    key_list = jax.random.split(jax.random.key(seed), 9)
    clips = normal_values(key_list[0], (CLIPS, D), 1.0, 6.0, ((0, 32),))
    captions = normal_values(key_list[1], (CAPTIONS, D), 1.0, 6.0, ((0, 32),))
    clip_bucket = draw_clip_bucket(jax.random.fold_in(key_list[8], 71), 0)
    clip_positive = draw_clip_positive(jax.random.fold_in(key_list[8], 71), 0)
    caption_bucket = draw_caption_bucket(jax.random.fold_in(key_list[8], 71), 0)
    bucket_owner = draw_bucket_owner(jax.random.fold_in(key_list[8], 71), 0)
    scale = jnp.clip(jnp.exp(jax.random.uniform(key_list[6], (1,), jnp.float32, math.log(0.02), math.log(0.06))), 0.02, 0.06)
    bias = jnp.clip(jax.random.uniform(key_list[7], (1,), jnp.float32, -4.0, -1.0), -4.0, -1.0)
    return dict(clips=clips, captions=captions, clip_bucket=clip_bucket, clip_positive=clip_positive, caption_bucket=caption_bucket, bucket_owner=bucket_owner, scale=scale, bias=bias)


def reference(clips, captions, clip_bucket, clip_positive, caption_bucket, bucket_owner, scale, bias):
    window = min(CLIPS, SLOTS * N_MEM)
    owner_group = bucket_owner[clip_bucket].astype(jnp.int32)
    order = jnp.argsort(owner_group, stable=True).astype(jnp.int32)
    sorted_group = owner_group[order]
    starts = jnp.searchsorted(sorted_group, jnp.arange(N_GRP, dtype=jnp.int32)).astype(jnp.int32)
    mult = scale[0]
    shift = bias[0]

    def one_group(carry, group):
        clip_acc, cap_acc = carry
        first = jnp.minimum(starts[group], CLIPS - window).astype(jnp.int32)
        rows = lax.dynamic_slice_in_dim(order, first, window)
        inside = lax.dynamic_slice_in_dim(sorted_group, first, window) == group
        block_x = clips[rows]
        block_b = jnp.where(inside, clip_bucket[rows], -1)
        block_p = clip_positive[rows]
        cap_first = (group * PANEL).astype(jnp.int32)
        block_y = lax.dynamic_slice_in_dim(captions, cap_first, PANEL, 0)
        block_cb = lax.dynamic_slice_in_dim(caption_bucket, cap_first, PANEL)
        ids = cap_first + jnp.arange(PANEL, dtype=jnp.int32)
        logits = mult * jnp.dot(block_x, block_y.T, preferred_element_type=jnp.float32) + shift
        sign = jnp.where(block_p[:, None] == ids[None, :], 1.0, -1.0).astype(jnp.float32)
        same = block_b[:, None] == block_cb[None, :]
        weight = jnp.where(same, -sign * jax.nn.sigmoid(-sign * logits), 0.0).astype(jnp.bfloat16)
        grad_x = jnp.dot(weight, block_y, preferred_element_type=jnp.float32)
        grad_y = jnp.dot(weight.T, block_x, preferred_element_type=jnp.float32)
        grad_x = jnp.where(inside[:, None], grad_x, 0.0)
        clip_acc = clip_acc.at[rows].add(grad_x)
        old = lax.dynamic_slice_in_dim(cap_acc, cap_first, PANEL, 0)
        cap_acc = lax.dynamic_update_slice_in_dim(cap_acc, old + grad_y, cap_first, 0)
        return (clip_acc, cap_acc), None

    start_carry = (jnp.zeros((CLIPS, D), jnp.float32), jnp.zeros((CAPTIONS, D), jnp.float32))
    (clip_grad, caption_grad), _ = lax.scan(one_group, start_carry, jnp.arange(N_GRP, dtype=jnp.int32))
    return clip_grad, caption_grad
```

```python
import functools

import jax
import jax.numpy as jnp
from jax import lax
from jax.experimental import pallas as pl
from jax.experimental.pallas import tpu as pltpu
from jax.sharding import PartitionSpec as P

MESH = pl.DeviceIdType.MESH
DEPTH = 4
META = 128
BF16 = jnp.bfloat16
F32 = jnp.float32


def iota(shape, dim):
    return lax.broadcasted_iota(jnp.int32, shape, dim)


def hot(condition):
    return jnp.where(condition, 1.0, 0.0).astype(BF16)


def dot_nn(a, b):
    return jnp.dot(a, b, preferred_element_type=F32)


def dot_nt(a, b):
    return lax.dot_general(a, b, (((1,), (1,)), ((), ())), preferred_element_type=F32)


def dot_tn(a, b):
    return lax.dot_general(a, b, (((0,), (0,)), ((), ())), preferred_element_type=F32)


def kernel(
    groups, members,
    owner_ref, scale_ref, bias_ref, bucket_ref, positive_ref, cap_bucket_ref, clips_ref, captions_ref,
    clip_grad_ref, cap_grad_ref,
    ybuf, xbuf, xsend, pack, wbuf, tsend, tback, cgrad, ysend, yback, zsend, zback,
    zs, zr, ys, yr, xs, xr, ts, tr, cys, cyr, czs, czr,
):
    clip_rows, width = clips_ref.shape
    cap_rows = captions_ref.shape[0]
    buckets = owner_ref.shape[0]
    depth = DEPTH
    side = members // depth
    cap = 2 * clip_rows // groups
    panel = cap_rows * members
    line = depth * cap_rows

    g = lax.axis_index("grp")
    m = lax.axis_index("mem")
    gx, gc = g // 2, g % 2
    mz, my = m // side, m % side
    xlen = groups // 2

    def grp_at(dx, dc):
        return (gx + dx + xlen) % xlen * 2 + (gc + dc + 2) % 2

    def mem_at(dz, dy):
        return (mz + dz + depth) % depth * side + (my + dy + side) % side

    barrier = pltpu.get_barrier_semaphore()
    for k in range(1, groups):
        pl.semaphore_signal(barrier, inc=1, device_id=(grp_at(k // 2, k % 2), m), device_id_type=MESH)
    for d in range(1, depth):
        pl.semaphore_signal(barrier, inc=1, device_id=(g, mem_at(d, 0)), device_id_type=MESH)
    for d in range(1, side):
        pl.semaphore_signal(barrier, inc=1, device_id=(g, mem_at(0, d)), device_id_type=MESH)

    rows = iota((META, cap_rows), 0)
    place = iota((META, cap_rows), 1)
    codes = jnp.where(rows == cap_bucket_ref[...], 4.0, 0.0)
    codes = jnp.where(rows == buckets + m, 1.0, codes)
    codes = jnp.where(rows == buckets + members + place, 1.0, codes).astype(BF16)
    eye = hot(iota((cap_rows, cap_rows), 0) == iota((cap_rows, cap_rows), 1))
    ybuf[pl.ds(0, cap_rows), pl.ds(0, width)] = captions_ref[...]
    ybuf[pl.ds(0, cap_rows), pl.ds(width, META)] = dot_nt(eye, codes).astype(BF16)

    bucket = bucket_ref[...]
    owner = jnp.zeros_like(bucket)
    for b in range(buckets):
        owner = jnp.where(bucket == b, owner_ref[b], owner)
    spot = positive_ref[...] - owner * panel
    height = max(16, groups)
    member = hot(iota((height, clip_rows), 0) == owner)
    upper = hot(iota((clip_rows, clip_rows), 0) < iota((clip_rows, clip_rows), 1))
    rank = jnp.sum(dot_nn(member, upper) * member.astype(F32), axis=0, keepdims=True)
    rows = iota((META, clip_rows), 0)
    clip_codes = hot(
        (rows == bucket)
        | (rows == buckets + spot // cap_rows)
        | (rows == buckets + members + spot % cap_rows)
    )
    slot = iota((cap, clip_rows), 0).astype(F32)

    pl.semaphore_wait(barrier, groups - 1 + depth - 1 + side - 1)

    def yrows(dy, dz):
        return pl.ds((dy * depth + dz) * cap_rows, cap_rows)

    def copy(src, dst, send, recv, device):
        return pltpu.make_async_remote_copy(
            src_ref=src, dst_ref=dst, send_sem=send, recv_sem=recv,
            device_id=device, device_id_type=MESH,
        )

    z_copies, y_copies = {}, {}
    for dz in range(1, depth):
        z_copies[dz] = copy(
            ybuf.at[yrows(0, 0)], ybuf.at[yrows(0, dz)], zs.at[dz - 1], zr.at[dz - 1], (g, mem_at(dz, 0))
        )
        z_copies[dz].start()

    def send_y(dz):
        for dy in range(1, side):
            n = (dy - 1) * depth + dz
            y_copies[n] = copy(
                ybuf.at[yrows(0, dz)], ybuf.at[yrows(dy, dz)], ys.at[n], yr.at[n], (g, mem_at(0, dy))
            )
            y_copies[n].start()

    send_y(0)

    def xrows(k):
        return pl.ds(k * cap, cap)

    x_copies, t_copies = {}, {}
    order = list(range(2, groups)) + [1, 0]
    for k in order:
        target = grp_at(k // 2, k % 2)
        choose = hot((slot == rank) & (owner == target))
        pack[xrows(k), :] = choose
        into = xsend if k else xbuf
        into[xrows(k), pl.ds(0, width)] = dot_nn(choose, clips_ref[...]).astype(BF16)
        into[xrows(k), pl.ds(width, META)] = dot_nt(choose, clip_codes).astype(BF16)
        if k:
            x_copies[k] = copy(xsend.at[xrows(k)], xbuf.at[xrows(k)], xs.at[k - 1], xr.at[k - 1], (target, m))
            x_copies[k].start()

    for dz in range(1, depth):
        z_copies[dz].wait_recv()
        send_y(dz)
    for n in y_copies:
        y_copies[n].wait_recv()

    mult, shift = scale_ref[0], bias_ref[0]

    def weigh(k):
        logits = mult * dot_nt(xbuf[xrows(k), pl.ds(0, width)], ybuf[:, pl.ds(0, width)]) + shift
        code = dot_nt(xbuf[xrows(k), pl.ds(width, META)], ybuf[:, pl.ds(width, META)])
        matched = code > 5.5
        level = jax.nn.sigmoid(jnp.where(matched, -logits, logits))
        weight = jnp.where(matched, -level, jnp.where(code > 3.5, level, 0.0))
        wbuf[xrows(k), :] = weight.astype(BF16)

    def give_back(k):
        total = dot_nn(wbuf[xrows(k), :], ybuf[:, pl.ds(0, width)]).astype(BF16)
        if k:
            tsend[xrows(k), :] = total
            t_copies[k] = copy(
                tsend.at[xrows(k)], tback.at[xrows(k)], ts.at[k - 1], tr.at[k - 1],
                (grp_at(-(k // 2), -(k % 2)), m),
            )
            t_copies[k].start()
        else:
            tback[xrows(k), :] = total

    for k in order:
        if k:
            x_copies[k].wait_recv()
        weigh(k)
        if k >= 2:
            give_back(k)

    cy_copies, cz_copies = {}, {}
    for dy in range(1, side):
        part = dot_tn(wbuf[:, pl.ds(dy * line, line)], xbuf[:, pl.ds(0, width)]).astype(BF16)
        ysend[pl.ds((dy - 1) * line, line), :] = part
        for dz in list(range(1, depth)) + [0]:
            n = (dy - 1) * depth + dz
            where = pl.ds(n * cap_rows, cap_rows)
            cy_copies[n] = copy(ysend.at[where], yback.at[where], cys.at[n], cyr.at[n], (g, mem_at(0, -dy)))
            cy_copies[n].start()
    give_back(1)
    cgrad[...] = dot_tn(wbuf[:, pl.ds(0, line)], xbuf[:, pl.ds(0, width)])
    give_back(0)

    def summed(dz):
        total = cgrad[pl.ds(dz * cap_rows, cap_rows), :]
        for dy in range(1, side):
            n = (dy - 1) * depth + dz
            cy_copies[n].wait_recv()
            total = total + yback[pl.ds(n * cap_rows, cap_rows), :].astype(F32)
        return total

    for dz in range(1, depth):
        where = pl.ds((dz - 1) * cap_rows, cap_rows)
        zsend[where, :] = summed(dz).astype(BF16)
        cz_copies[dz] = copy(
            zsend.at[where], zback.at[where], czs.at[dz - 1], czr.at[dz - 1], (g, mem_at(-dz, 0))
        )
        cz_copies[dz].start()
    cap_total = summed(0)

    clip_total = dot_tn(pack[xrows(0), :], tback[xrows(0), :])
    for k in [1] + list(range(2, groups)):
        t_copies[k].wait_recv()
        clip_total = clip_total + dot_tn(pack[xrows(k), :], tback[xrows(k), :])
    clip_grad_ref[...] = clip_total

    for dz in range(1, depth):
        cz_copies[dz].wait_recv()
        cap_total = cap_total + zback[pl.ds((dz - 1) * cap_rows, cap_rows), :].astype(F32)
    cap_grad_ref[...] = cap_total

    for copies in (z_copies, y_copies, x_copies, t_copies, cy_copies, cz_copies):
        for n in copies:
            copies[n].wait_send()


def body(clips, captions, clip_bucket, clip_positive, caption_bucket, bucket_owner, scale, bias):
    groups = lax.axis_size("grp")
    members = lax.axis_size("mem")
    clip_rows, width = clips.shape
    cap_rows = captions.shape[0]
    side = members // DEPTH
    slots = 2 * clip_rows
    panel = cap_rows * members
    line = DEPTH * cap_rows
    smem = pl.BlockSpec(memory_space=pltpu.SMEM)
    vmem = pl.BlockSpec(memory_space=pltpu.VMEM)
    dma = pltpu.SemaphoreType.DMA
    clip_grad, caption_grad = pl.pallas_call(
        functools.partial(kernel, groups, members),
        out_shape=(
            jax.ShapeDtypeStruct((clip_rows, width), F32),
            jax.ShapeDtypeStruct((cap_rows, width), F32),
        ),
        in_specs=[smem] * 3 + [vmem] * 5,
        out_specs=(vmem, vmem),
        scratch_shapes=[
            pltpu.VMEM((panel, width + META), BF16),
            pltpu.VMEM((slots, width + META), BF16),
            pltpu.VMEM((slots, width + META), BF16),
            pltpu.VMEM((slots, clip_rows), BF16),
            pltpu.VMEM((slots, panel), BF16),
            pltpu.VMEM((slots, width), BF16),
            pltpu.VMEM((slots, width), BF16),
            pltpu.VMEM((line, width), F32),
            pltpu.VMEM((panel - line, width), BF16),
            pltpu.VMEM((panel - line, width), BF16),
            pltpu.VMEM((line - cap_rows, width), BF16),
            pltpu.VMEM((line - cap_rows, width), BF16),
            dma((DEPTH - 1,)), dma((DEPTH - 1,)),
            dma(((side - 1) * DEPTH,)), dma(((side - 1) * DEPTH,)),
            dma((groups - 1,)), dma((groups - 1,)),
            dma((groups - 1,)), dma((groups - 1,)),
            dma(((side - 1) * DEPTH,)), dma(((side - 1) * DEPTH,)),
            dma((DEPTH - 1,)), dma((DEPTH - 1,)),
        ],
        compiler_params=pltpu.CompilerParams(
            collective_id=0, has_side_effects=True, vmem_limit_bytes=48 * 1024 * 1024
        ),
    )(
        bucket_owner, scale, bias,
        clip_bucket.reshape(1, clip_rows), clip_positive.reshape(1, clip_rows), caption_bucket.reshape(1, cap_rows),
        clips, captions,
    )
    return (clip_grad, caption_grad)


def solution(mesh):
    placed = (
        P(("grp", "mem"), None),
        P(("grp", "mem"), None),
        P(("grp", "mem")),
        P(("grp", "mem")),
        P(("grp", "mem")),
        P(),
        P(),
        P(),
    )
    return jax.shard_map(
        body,
        mesh=mesh,
        in_specs=placed,
        out_specs=(P(("grp", "mem"), None), P(("grp", "mem"), None)),
        check_vma=False,
    )
```

```python
import functools

import jax
import jax.numpy as jnp
from jax import lax
from jax.experimental import pallas as pl
from jax.experimental.pallas import tpu as pltpu
from jax.sharding import PartitionSpec as P

MESH = pl.DeviceIdType.MESH
DEPTH = 4
META = 128
BF16 = jnp.bfloat16
F32 = jnp.float32


def iota(shape, dim):
    return lax.broadcasted_iota(jnp.int32, shape, dim)


def hot(condition):
    return jnp.where(condition, 1.0, 0.0).astype(BF16)


def dot_nn(a, b):
    return jnp.dot(a, b, preferred_element_type=F32)


def dot_nt(a, b):
    return lax.dot_general(a, b, (((1,), (1,)), ((), ())), preferred_element_type=F32)


def dot_tn(a, b):
    return lax.dot_general(a, b, (((0,), (0,)), ((), ())), preferred_element_type=F32)


def kernel(
    groups, members,
    owner_hbm, scale_hbm, bias_hbm, bucket_hbm, positive_hbm, cap_bucket_hbm, clips_hbm, captions_hbm,
    clip_grad_ref, cap_grad_ref,
    owner_ref, scale_ref, bias_ref, bucket_ref, positive_ref, cap_bucket_ref, clips_ref,
    ybuf, ymeta, ycodes, xbuf, xsend, xmeta, xmeta_send, pack,
    wbuf, tsend, tback, cgrad, ysend, yback, zsend, zback,
    local, rs, rr, ls, lr, ys, yr, ms, mr, xs, xr, xms, xmr, ts, tr, cys, cyr, czs, czr,
):
    clip_rows, width = clips_ref.shape
    cap_rows = cap_bucket_ref.shape[1]
    buckets = owner_ref.shape[0]
    depth = DEPTH
    side = members // depth
    cap = 2 * clip_rows // groups
    panel = cap_rows * members
    line = depth * cap_rows

    g = lax.axis_index("grp")
    m = lax.axis_index("mem")
    gx, gc = g // 2, g % 2
    mz, my = m // side, m % side
    xlen = groups // 2

    def grp_at(dx, dc):
        return (gx + dx + xlen) % xlen * 2 + (gc + dc + 2) % 2

    def mem_at(dz, dy):
        return (mz + dz + depth) % depth * side + (my + dy + side) % side

    def yrows(dy, dz):
        return pl.ds((dy * depth + dz) * cap_rows, cap_rows)

    def xrows(k):
        return pl.ds(k * cap, cap)

    loads = [
        pltpu.make_async_copy(src, dst, local.at[n])
        for n, (src, dst) in enumerate((
            (captions_hbm, ybuf.at[yrows(0, 0)]),
            (cap_bucket_hbm, cap_bucket_ref),
            (bucket_hbm, bucket_ref),
            (positive_hbm, positive_ref),
            (owner_hbm, owner_ref),
            (scale_hbm, scale_ref),
            (bias_hbm, bias_ref),
            (clips_hbm, clips_ref),
        ))
    ]
    for load in loads:
        load.start()

    barrier = pltpu.get_barrier_semaphore()
    others = [(dy, dz) for dy in range(side) for dz in range(depth)][1:]
    for k in range(1, groups):
        pl.semaphore_signal(barrier, inc=1, device_id=(grp_at(k // 2, k % 2), m), device_id_type=MESH)
    for dy, dz in others:
        pl.semaphore_signal(barrier, inc=1, device_id=(g, mem_at(dz, dy)), device_id_type=MESH)

    for load in loads[:-1]:
        load.wait()

    tile = 8
    cap_bucket = jnp.broadcast_to(cap_bucket_ref[...], (tile, cap_rows))
    ymeta[pl.ds(0, tile), :] = jnp.zeros((tile, META), jnp.int32)
    ymeta[pl.ds(0, tile), pl.ds(0, cap_rows)] = cap_bucket
    xmeta_send[...] = jnp.zeros_like(xmeta_send)

    def copy(src, dst, send, recv, device):
        return pltpu.make_async_remote_copy(
            src_ref=src, dst_ref=dst, send_sem=send, recv_sem=recv,
            device_id=device, device_id_type=MESH,
        )

    def right(s):
        return copy(
            ybuf.at[yrows(0, s - 1)], ybuf.at[yrows(0, s)], rs.at[s - 1], rr.at[s - 1], (g, mem_at(1, 0))
        )

    def left(s):
        return copy(
            ybuf.at[yrows(0, (depth - s + 1) % depth)], ybuf.at[yrows(0, depth - s)],
            ls.at[s - 1], lr.at[s - 1], (g, mem_at(-1, 0)),
        )

    def over_y(dy, dz):
        n = (dy - 1) * depth + dz
        return copy(ybuf.at[yrows(0, dz)], ybuf.at[yrows(dy, dz)], ys.at[n], yr.at[n], (g, mem_at(0, dy)))

    def send_y(dz):
        for dy in range(1, side):
            over_y(dy, dz).start()

    def hop(s):
        @pl.when(mz >= s)
        def _():
            right(s).wait_recv()
            if s + 1 < depth:
                @pl.when(mz + 1 < depth)
                def _():
                    right(s + 1).start()
            send_y(s)

        @pl.when(mz + s < depth)
        def _():
            left(s).wait_recv()
            if s + 1 < depth:
                @pl.when(mz >= 1)
                def _():
                    left(s + 1).start()
            send_y(depth - s)

    pl.semaphore_wait(barrier, groups - 1 + members - 1)

    @pl.when(mz + 1 < depth)
    def _():
        right(1).start()

    @pl.when(mz >= 1)
    def _():
        left(1).start()

    send_y(0)
    m_copies = {}
    for n, (dy, dz) in enumerate(others):
        there = pl.ds((dy * depth + dz) * tile, tile)
        m_copies[n] = copy(ymeta.at[pl.ds(0, tile)], ymeta.at[there], ms.at[n], mr.at[n], (g, mem_at(dz, dy)))
        m_copies[n].start()

    bucket = bucket_ref[...]
    owner = jnp.zeros_like(bucket)
    for b in range(buckets):
        owner = jnp.where(bucket == b, owner_ref[b], owner)
    spot = positive_ref[...] - owner * panel
    height = max(16, groups)
    member = hot(iota((height, clip_rows), 0) == owner)
    upper = hot(iota((clip_rows, clip_rows), 0) < iota((clip_rows, clip_rows), 1))
    rank = jnp.sum(dot_nn(member, upper) * member.astype(F32), axis=0, keepdims=True)
    rows = iota((16, clip_rows), 0)
    facts = jnp.where(rows == 0, bucket + 1, jnp.where(rows == 1, spot // cap_rows, spot % cap_rows))
    facts = facts.astype(F32).astype(BF16)
    slot = iota((cap, clip_rows), 0).astype(F32)
    loads[-1].wait()

    x_copies, xm_copies, t_copies = {}, {}, {}

    def pack_for(k):
        target = grp_at(k // 2, k % 2)
        choose = hot((slot == rank) & (owner == target))
        pack[xrows(k), :] = choose
        into, facts_into = (xsend, xmeta_send) if k else (xbuf, xmeta)
        facts_into[pl.ds(k * tile, tile), pl.ds(0, cap)] = dot_nt(facts, choose)[:tile]
        into[xrows(k), :] = dot_nn(choose, clips_ref[...]).astype(BF16)
        if k:
            trows = pl.ds(k * tile, tile)
            x_copies[k] = copy(xsend.at[xrows(k)], xbuf.at[xrows(k)], xs.at[k - 1], xr.at[k - 1], (target, m))
            x_copies[k].start()
            xm_copies[k] = copy(
                xmeta_send.at[trows], xmeta.at[trows], xms.at[k - 1], xmr.at[k - 1], (target, m)
            )
            xm_copies[k].start()

    far = list(range(2, groups))
    for k in far:
        pack_for(k)
    hop(1)
    pack_for(1)
    pack_for(0)
    hop(2)

    for n in m_copies:
        m_copies[n].wait_recv()
    rows = iota((META, cap_rows), 0)
    place = iota((META, cap_rows), 1)
    for dy in range(side):
        for dz in range(depth):
            j = dy * depth + dz
            codes = jnp.where(rows == ymeta[pl.ds(j * tile, 1), pl.ds(0, cap_rows)], 4.0, 0.0)
            codes = jnp.where(rows == buckets + mem_at(-dz, -dy), 1.0, codes)
            codes = jnp.where(rows == buckets + members + place, 1.0, codes)
            ycodes[:, yrows(dy, dz)] = codes.astype(BF16)
    mult, shift = scale_ref[0], bias_ref[0]
    rows_x = iota((META, cap), 0).astype(F32)

    def weigh(k, dy):
        there = pl.ds(dy * line, line)
        fact = [xmeta[pl.ds(k * tile + n, 1), pl.ds(0, cap)] for n in range(3)]
        codes = hot(
            (rows_x == fact[0] - 1.0)
            | (rows_x == fact[1] + buckets)
            | (rows_x == fact[2] + (buckets + members))
        )
        logits = mult * dot_nt(xbuf[xrows(k), :], ybuf[there, :]) + shift
        code = dot_tn(codes, ycodes[:, there])
        matched = code > 5.5
        level = jax.nn.sigmoid(jnp.where(matched, -logits, logits))
        weight = jnp.where(matched, -level, jnp.where(code > 3.5, level, 0.0))
        wbuf[xrows(k), there] = weight.astype(BF16)

    def arrive(k):
        x_copies[k].wait_recv()
        xm_copies[k].wait_recv()

    def give_back(k):
        total = dot_nn(wbuf[xrows(k), :], ybuf[...]).astype(BF16)
        if k:
            tsend[xrows(k), :] = total
            t_copies[k] = copy(
                tsend.at[xrows(k)], tback.at[xrows(k)], ts.at[k - 1], tr.at[k - 1],
                (grp_at(-(k // 2), -(k % 2)), m),
            )
            t_copies[k].start()
        else:
            tback[xrows(k), :] = total

    for s in range(3, depth):
        hop(s)
    weigh(0, 0)
    arrive(1)
    weigh(1, 0)
    for k in far[:-1]:
        arrive(k)
        weigh(k, 0)
    for dy in range(1, side):
        for dz in range(depth):
            over_y(dy, dz).wait_recv()
        for k in far[:-1]:
            weigh(k, dy)
    for k in far[:-1]:
        give_back(k)
    arrive(far[-1])
    for dy in range(side):
        weigh(far[-1], dy)
    give_back(far[-1])
    for dy in range(1, side):
        weigh(1, dy)
        weigh(0, dy)

    cy_copies, cz_copies = {}, {}
    for dy in range(1, side):
        part = dot_tn(wbuf[:, pl.ds(dy * line, line)], xbuf[...]).astype(BF16)
        ysend[pl.ds((dy - 1) * line, line), :] = part
        for dz in [2, 1, 3, 0]:
            n = (dy - 1) * depth + dz
            where = pl.ds(n * cap_rows, cap_rows)
            cy_copies[n] = copy(ysend.at[where], yback.at[where], cys.at[n], cyr.at[n], (g, mem_at(0, -dy)))
            cy_copies[n].start()
    give_back(1)
    cgrad[...] = dot_tn(wbuf[:, pl.ds(0, line)], xbuf[...])
    give_back(0)

    def summed(dz):
        total = cgrad[pl.ds(dz * cap_rows, cap_rows), :]
        for dy in range(1, side):
            n = (dy - 1) * depth + dz
            cy_copies[n].wait_recv()
            total = total + yback[pl.ds(n * cap_rows, cap_rows), :].astype(F32)
        return total

    for dz in [2, 1, 3]:
        where = pl.ds((dz - 1) * cap_rows, cap_rows)
        zsend[where, :] = summed(dz).astype(BF16)
        cz_copies[dz] = copy(
            zsend.at[where], zback.at[where], czs.at[dz - 1], czr.at[dz - 1], (g, mem_at(-dz, 0))
        )
        cz_copies[dz].start()
    cap_grad_ref[...] = summed(0)

    t_copies[1].wait_recv()
    near = pl.ds(0, 2 * cap)
    clip_grad_ref[...] = dot_tn(pack[near, :], tback[near, :])
    for k in far:
        t_copies[k].wait_recv()
        clip_grad_ref[...] += dot_tn(pack[xrows(k), :], tback[xrows(k), :])

    for dz in cz_copies:
        cz_copies[dz].wait_recv()
        cap_grad_ref[...] += zback[pl.ds((dz - 1) * cap_rows, cap_rows), :].astype(F32)

    for s in range(1, depth):
        @pl.when((mz + 1 < depth) & (mz >= s - 1))
        def _():
            right(s).wait_send()

        @pl.when((mz >= 1) & (mz + s - 1 < depth))
        def _():
            left(s).wait_send()

    for dy in range(1, side):
        for dz in range(depth):
            over_y(dy, dz).wait_send()
    for copies in (m_copies, x_copies, xm_copies, t_copies, cy_copies, cz_copies):
        for n in copies:
            copies[n].wait_send()


def body(clips, captions, clip_bucket, clip_positive, caption_bucket, bucket_owner, scale, bias):
    groups = lax.axis_size("grp")
    members = lax.axis_size("mem")
    clip_rows, width = clips.shape
    cap_rows = captions.shape[0]
    side = members // DEPTH
    slots = 2 * clip_rows
    panel = cap_rows * members
    line = DEPTH * cap_rows
    hbm = pl.BlockSpec(memory_space=pltpu.HBM)
    vmem = pl.BlockSpec(memory_space=pltpu.VMEM)
    dma = pltpu.SemaphoreType.DMA
    pairs = lambda n: [dma((n,)), dma((n,))]
    ysteps = (side - 1) * DEPTH
    clip_grad, caption_grad = pl.pallas_call(
        functools.partial(kernel, groups, members),
        out_shape=(
            jax.ShapeDtypeStruct((clip_rows, width), F32),
            jax.ShapeDtypeStruct((cap_rows, width), F32),
        ),
        in_specs=[hbm] * 8,
        out_specs=(vmem, vmem),
        scratch_shapes=[
            pltpu.SMEM(bucket_owner.shape, jnp.int32),
            pltpu.SMEM((1,), F32),
            pltpu.SMEM((1,), F32),
            pltpu.VMEM((1, clip_rows), jnp.int32),
            pltpu.VMEM((1, clip_rows), jnp.int32),
            pltpu.VMEM((1, cap_rows), jnp.int32),
            pltpu.VMEM((clip_rows, width), BF16),
            pltpu.VMEM((panel, width), BF16),
            pltpu.VMEM((8 * members, META), jnp.int32),
            pltpu.VMEM((META, panel), BF16),
            pltpu.VMEM((slots, width), BF16),
            pltpu.VMEM((slots, width), BF16),
            pltpu.VMEM((8 * groups, META), F32),
            pltpu.VMEM((8 * groups, META), F32),
            pltpu.VMEM((slots, clip_rows), BF16),
            pltpu.VMEM((slots, panel), BF16),
            pltpu.VMEM((slots, width), BF16),
            pltpu.VMEM((slots, width), BF16),
            pltpu.VMEM((line, width), F32),
            pltpu.VMEM((panel - line, width), BF16),
            pltpu.VMEM((panel - line, width), BF16),
            pltpu.VMEM((line - cap_rows, width), BF16),
            pltpu.VMEM((line - cap_rows, width), BF16),
            dma((8,)),
            *pairs(DEPTH - 1), *pairs(DEPTH - 1), *pairs(ysteps), *pairs(members - 1),
            *pairs(groups - 1), *pairs(groups - 1), *pairs(groups - 1),
            *pairs(ysteps), *pairs(DEPTH - 1),
        ],
        compiler_params=pltpu.CompilerParams(
            collective_id=0, has_side_effects=True, vmem_limit_bytes=63 * 1024 * 1024
        ),
    )(
        bucket_owner, scale, bias,
        clip_bucket.reshape(1, clip_rows), clip_positive.reshape(1, clip_rows), caption_bucket.reshape(1, cap_rows),
        clips, captions,
    )
    return (clip_grad, caption_grad)


def solution(mesh):
    placed = (
        P(("grp", "mem"), None),
        P(("grp", "mem"), None),
        P(("grp", "mem")),
        P(("grp", "mem")),
        P(("grp", "mem")),
        P(),
        P(),
        P(),
    )
    return jax.shard_map(
        body,
        mesh=mesh,
        in_specs=placed,
        out_specs=(P(("grp", "mem"), None), P(("grp", "mem"), None)),
        check_vma=False,
    )
```

```python
import functools

import jax
import jax.numpy as jnp
from jax import lax
from jax.experimental import pallas as pl
from jax.experimental.pallas import tpu as pltpu
from jax.sharding import PartitionSpec as P

MESH = pl.DeviceIdType.MESH
DEPTH = 4
META = 128
BF16 = jnp.bfloat16
F32 = jnp.float32


def iota(shape, dim):
    return lax.broadcasted_iota(jnp.int32, shape, dim)


def hot(condition):
    return jnp.where(condition, 1.0, 0.0).astype(BF16)


def dot_nn(a, b):
    return jnp.dot(a, b, preferred_element_type=F32)


def dot_nt(a, b):
    return lax.dot_general(a, b, (((1,), (1,)), ((), ())), preferred_element_type=F32)


def dot_tn(a, b):
    return lax.dot_general(a, b, (((0,), (0,)), ((), ())), preferred_element_type=F32)


def kernel(
    groups, members,
    owner_hbm, scale_hbm, bias_hbm, bucket_hbm, positive_hbm, cap_bucket_hbm, clips_hbm, captions_hbm,
    clip_grad_ref, cap_grad_ref,
    owner_ref, scale_ref, bias_ref, bucket_ref, positive_ref, cap_bucket_ref, clips_ref,
    ybuf, ymeta, ycodes, xbuf, xsend, xmeta, xmeta_send, pack,
    wbuf, tsend, tback, cgrad, ysend, yback, zsend, zback,
    local, rs, rr, ls, lr, ys, yr, ms, mr, xs, xr, xms, xmr, ts, tr, cys, cyr, czs, czr,
):
    clip_rows, width = clips_ref.shape
    cap_rows = cap_bucket_ref.shape[1]
    buckets = owner_ref.shape[0]
    depth = DEPTH
    side = members // depth
    cap = 2 * clip_rows // groups
    panel = cap_rows * members
    line = depth * cap_rows

    g = lax.axis_index("grp")
    m = lax.axis_index("mem")
    gx, gc = g // 2, g % 2
    mz, my = m // side, m % side
    xlen = groups // 2

    def grp_at(dx, dc):
        return (gx + dx + xlen) % xlen * 2 + (gc + dc + 2) % 2

    def mem_at(dz, dy):
        return (mz + dz + depth) % depth * side + (my + dy + side) % side

    def yrows(dy, dz):
        return pl.ds((dy * depth + dz) * cap_rows, cap_rows)

    def xrows(k):
        return pl.ds(k * cap, cap)

    loads = [
        pltpu.make_async_copy(src, dst, local.at[n])
        for n, (src, dst) in enumerate((
            (captions_hbm, ybuf.at[yrows(0, 0)]),
            (cap_bucket_hbm, cap_bucket_ref),
            (bucket_hbm, bucket_ref),
            (positive_hbm, positive_ref),
            (owner_hbm, owner_ref),
            (scale_hbm, scale_ref),
            (bias_hbm, bias_ref),
            (clips_hbm, clips_ref),
        ))
    ]
    for load in loads:
        load.start()

    barrier = pltpu.get_barrier_semaphore()
    others = [(dy, dz) for dy in range(side) for dz in range(depth)][1:]
    for k in range(1, groups):
        pl.semaphore_signal(barrier, inc=1, device_id=(grp_at(k // 2, k % 2), m), device_id_type=MESH)
    for dy, dz in others:
        pl.semaphore_signal(barrier, inc=1, device_id=(g, mem_at(dz, dy)), device_id_type=MESH)

    for load in loads[:-1]:
        load.wait()

    tile = 8
    cap_bucket = jnp.broadcast_to(cap_bucket_ref[...], (tile, cap_rows))
    ymeta[pl.ds(0, tile), :] = jnp.zeros((tile, META), jnp.int32)
    ymeta[pl.ds(0, tile), pl.ds(0, cap_rows)] = cap_bucket
    xmeta_send[...] = jnp.zeros_like(xmeta_send)

    def copy(src, dst, send, recv, device):
        return pltpu.make_async_remote_copy(
            src_ref=src, dst_ref=dst, send_sem=send, recv_sem=recv,
            device_id=device, device_id_type=MESH,
        )

    def right(s):
        return copy(
            ybuf.at[yrows(0, s - 1)], ybuf.at[yrows(0, s)], rs.at[s - 1], rr.at[s - 1], (g, mem_at(1, 0))
        )

    def left(s):
        return copy(
            ybuf.at[yrows(0, (depth - s + 1) % depth)], ybuf.at[yrows(0, depth - s)],
            ls.at[s - 1], lr.at[s - 1], (g, mem_at(-1, 0)),
        )

    def over_y(dy, dz):
        n = (dy - 1) * depth + dz
        return copy(ybuf.at[yrows(0, dz)], ybuf.at[yrows(dy, dz)], ys.at[n], yr.at[n], (g, mem_at(0, dy)))

    def send_y(dz):
        for dy in range(1, side):
            over_y(dy, dz).start()

    def hop(s):
        @pl.when(mz >= s)
        def _():
            right(s).wait_recv()
            if s + 1 < depth:
                @pl.when(mz + 1 < depth)
                def _():
                    right(s + 1).start()
            send_y(s)

        @pl.when(mz + s < depth)
        def _():
            left(s).wait_recv()
            if s + 1 < depth:
                @pl.when(mz >= 1)
                def _():
                    left(s + 1).start()
            send_y(depth - s)

    pl.semaphore_wait(barrier, groups - 1 + members - 1)

    @pl.when(mz + 1 < depth)
    def _():
        right(1).start()

    @pl.when(mz >= 1)
    def _():
        left(1).start()

    send_y(0)
    m_copies = {}
    for n, (dy, dz) in enumerate(others):
        there = pl.ds((dy * depth + dz) * tile, tile)
        m_copies[n] = copy(ymeta.at[pl.ds(0, tile)], ymeta.at[there], ms.at[n], mr.at[n], (g, mem_at(dz, dy)))
        m_copies[n].start()

    bucket = bucket_ref[...]
    owner = jnp.zeros_like(bucket)
    for b in range(buckets):
        owner = jnp.where(bucket == b, owner_ref[b], owner)
    spot = positive_ref[...] - owner * panel
    height = max(16, groups)
    member = hot(iota((height, clip_rows), 0) == owner)
    upper = hot(iota((clip_rows, clip_rows), 0) < iota((clip_rows, clip_rows), 1))
    rank = jnp.sum(dot_nn(member, upper) * member.astype(F32), axis=0, keepdims=True)
    rows = iota((16, clip_rows), 0)
    facts = jnp.where(rows == 0, bucket + 1, jnp.where(rows == 1, spot // cap_rows, spot % cap_rows))
    facts = facts.astype(F32).astype(BF16)
    slot = iota((cap, clip_rows), 0).astype(F32)
    loads[-1].wait()

    x_copies, xm_copies, t_copies = {}, {}, {}

    def pack_for(k):
        target = grp_at(k // 2, k % 2)
        choose = hot((slot == rank) & (owner == target))
        pack[xrows(k), :] = choose
        into, facts_into = (xsend, xmeta_send) if k else (xbuf, xmeta)
        facts_into[pl.ds(k * tile, tile), pl.ds(0, cap)] = dot_nt(facts, choose)[:tile]
        into[xrows(k), :] = dot_nn(choose, clips_ref[...]).astype(BF16)
        if k:
            trows = pl.ds(k * tile, tile)
            x_copies[k] = copy(xsend.at[xrows(k)], xbuf.at[xrows(k)], xs.at[k - 1], xr.at[k - 1], (target, m))
            x_copies[k].start()
            xm_copies[k] = copy(
                xmeta_send.at[trows], xmeta.at[trows], xms.at[k - 1], xmr.at[k - 1], (target, m)
            )
            xm_copies[k].start()

    far = list(range(2, groups))
    for k in far:
        pack_for(k)
    hop(1)
    pack_for(1)
    pack_for(0)
    hop(2)

    for n in m_copies:
        m_copies[n].wait_recv()
    rows = iota((META, cap_rows), 0)
    place = iota((META, cap_rows), 1)
    for dy in range(side):
        for dz in range(depth):
            j = dy * depth + dz
            codes = jnp.where(rows == ymeta[pl.ds(j * tile, 1), pl.ds(0, cap_rows)], 4.0, 0.0)
            codes = jnp.where(rows == buckets + mem_at(-dz, -dy), 1.0, codes)
            codes = jnp.where(rows == buckets + members + place, 1.0, codes)
            ycodes[:, yrows(dy, dz)] = codes.astype(BF16)
    mult, shift = scale_ref[0], bias_ref[0]
    rows_x = iota((META, cap), 0).astype(F32)

    def weigh(k, dy):
        there = pl.ds(dy * line, line)
        fact = [xmeta[pl.ds(k * tile + n, 1), pl.ds(0, cap)] for n in range(3)]
        codes = hot(
            (rows_x == fact[0] - 1.0)
            | (rows_x == fact[1] + buckets)
            | (rows_x == fact[2] + (buckets + members))
        )
        logits = mult * dot_nt(xbuf[xrows(k), :], ybuf[there, :]) + shift
        code = dot_tn(codes, ycodes[:, there])
        matched = code > 5.5
        level = jax.nn.sigmoid(jnp.where(matched, -logits, logits))
        weight = jnp.where(matched, -level, jnp.where(code > 3.5, level, 0.0))
        wbuf[xrows(k), there] = weight.astype(BF16)

    def arrive(k):
        x_copies[k].wait_recv()
        xm_copies[k].wait_recv()

    def give_back(k):
        total = dot_nn(wbuf[xrows(k), :], ybuf[...]).astype(BF16)
        if k:
            tsend[xrows(k), :] = total
            t_copies[k] = copy(
                tsend.at[xrows(k)], tback.at[xrows(k)], ts.at[k - 1], tr.at[k - 1],
                (grp_at(-(k // 2), -(k % 2)), m),
            )
            t_copies[k].start()
        else:
            tback[xrows(k), :] = total

    for s in range(3, depth):
        hop(s)
    weigh(0, 0)
    arrive(1)
    weigh(1, 0)
    for k in far[:-1]:
        arrive(k)
        weigh(k, 0)
    for dy in range(1, side):
        for dz in range(depth):
            over_y(dy, dz).wait_recv()
        for k in far[:-1]:
            weigh(k, dy)
    for k in far[:-1]:
        give_back(k)
    arrive(far[-1])
    for dy in range(side):
        weigh(far[-1], dy)
    give_back(far[-1])
    for dy in range(1, side):
        weigh(1, dy)
        weigh(0, dy)

    cy_copies, cz_copies = {}, {}
    for dy in range(1, side):
        part = dot_tn(wbuf[:, pl.ds(dy * line, line)], xbuf[...]).astype(BF16)
        ysend[pl.ds((dy - 1) * line, line), :] = part
        for dz in [2, 1, 3, 0]:
            n = (dy - 1) * depth + dz
            where = pl.ds(n * cap_rows, cap_rows)
            cy_copies[n] = copy(ysend.at[where], yback.at[where], cys.at[n], cyr.at[n], (g, mem_at(0, -dy)))
            cy_copies[n].start()
    give_back(1)
    cgrad[...] = dot_tn(wbuf[:, pl.ds(0, line)], xbuf[...])
    give_back(0)

    def summed(dz):
        total = cgrad[pl.ds(dz * cap_rows, cap_rows), :]
        for dy in range(1, side):
            n = (dy - 1) * depth + dz
            cy_copies[n].wait_recv()
            total = total + yback[pl.ds(n * cap_rows, cap_rows), :].astype(F32)
        return total

    for dz in [2, 1, 3]:
        where = pl.ds((dz - 1) * cap_rows, cap_rows)
        zsend[where, :] = summed(dz).astype(BF16)
        cz_copies[dz] = copy(
            zsend.at[where], zback.at[where], czs.at[dz - 1], czr.at[dz - 1], (g, mem_at(-dz, 0))
        )
        cz_copies[dz].start()
    cap_grad_ref[...] = summed(0)

    t_copies[1].wait_recv()
    near = pl.ds(0, 2 * cap)
    clip_grad_ref[...] = dot_tn(pack[near, :], tback[near, :]).astype(BF16)
    for k in far:
        t_copies[k].wait_recv()
        clip_grad_ref[...] += dot_tn(pack[xrows(k), :], tback[xrows(k), :]).astype(BF16)

    for dz in cz_copies:
        cz_copies[dz].wait_recv()
        cap_grad_ref[...] += zback[pl.ds((dz - 1) * cap_rows, cap_rows), :].astype(F32)

    for s in range(1, depth):
        @pl.when((mz + 1 < depth) & (mz >= s - 1))
        def _():
            right(s).wait_send()

        @pl.when((mz >= 1) & (mz + s - 1 < depth))
        def _():
            left(s).wait_send()

    for dy in range(1, side):
        for dz in range(depth):
            over_y(dy, dz).wait_send()
    for copies in (m_copies, x_copies, xm_copies, t_copies, cy_copies, cz_copies):
        for n in copies:
            copies[n].wait_send()


def body(clips, captions, clip_bucket, clip_positive, caption_bucket, bucket_owner, scale, bias):
    groups = lax.axis_size("grp")
    members = lax.axis_size("mem")
    clip_rows, width = clips.shape
    cap_rows = captions.shape[0]
    side = members // DEPTH
    slots = 2 * clip_rows
    panel = cap_rows * members
    line = DEPTH * cap_rows
    hbm = pl.BlockSpec(memory_space=pltpu.HBM)
    vmem = pl.BlockSpec(memory_space=pltpu.VMEM)
    dma = pltpu.SemaphoreType.DMA
    pairs = lambda n: [dma((n,)), dma((n,))]
    ysteps = (side - 1) * DEPTH
    clip_grad, caption_grad = pl.pallas_call(
        functools.partial(kernel, groups, members),
        out_shape=(
            jax.ShapeDtypeStruct((clip_rows, width), BF16),
            jax.ShapeDtypeStruct((cap_rows, width), F32),
        ),
        in_specs=[hbm] * 8,
        out_specs=(vmem, vmem),
        scratch_shapes=[
            pltpu.SMEM(bucket_owner.shape, jnp.int32),
            pltpu.SMEM((1,), F32),
            pltpu.SMEM((1,), F32),
            pltpu.VMEM((1, clip_rows), jnp.int32),
            pltpu.VMEM((1, clip_rows), jnp.int32),
            pltpu.VMEM((1, cap_rows), jnp.int32),
            pltpu.VMEM((clip_rows, width), BF16),
            pltpu.VMEM((panel, width), BF16),
            pltpu.VMEM((8 * members, META), jnp.int32),
            pltpu.VMEM((META, panel), BF16),
            pltpu.VMEM((slots, width), BF16),
            pltpu.VMEM((slots, width), BF16),
            pltpu.VMEM((8 * groups, META), F32),
            pltpu.VMEM((8 * groups, META), F32),
            pltpu.VMEM((slots, clip_rows), BF16),
            pltpu.VMEM((slots, panel), BF16),
            pltpu.VMEM((slots, width), BF16),
            pltpu.VMEM((slots, width), BF16),
            pltpu.VMEM((line, width), F32),
            pltpu.VMEM((panel - line, width), BF16),
            pltpu.VMEM((panel - line, width), BF16),
            pltpu.VMEM((line - cap_rows, width), BF16),
            pltpu.VMEM((line - cap_rows, width), BF16),
            dma((8,)),
            *pairs(DEPTH - 1), *pairs(DEPTH - 1), *pairs(ysteps), *pairs(members - 1),
            *pairs(groups - 1), *pairs(groups - 1), *pairs(groups - 1),
            *pairs(ysteps), *pairs(DEPTH - 1),
        ],
        compiler_params=pltpu.CompilerParams(
            collective_id=0, has_side_effects=True, vmem_limit_bytes=63 * 1024 * 1024
        ),
    )(
        bucket_owner, scale, bias,
        clip_bucket.reshape(1, clip_rows), clip_positive.reshape(1, clip_rows), caption_bucket.reshape(1, cap_rows),
        clips, captions,
    )
    return (clip_grad.astype(F32), caption_grad)


def solution(mesh):
    placed = (
        P(("grp", "mem"), None),
        P(("grp", "mem"), None),
        P(("grp", "mem")),
        P(("grp", "mem")),
        P(("grp", "mem")),
        P(),
        P(),
        P(),
    )
    return jax.shard_map(
        body,
        mesh=mesh,
        in_specs=placed,
        out_specs=(P(("grp", "mem"), None), P(("grp", "mem"), None)),
        check_vma=False,
    )
```
